128 devices in a mesh: row: 8 (over x, y_lo), col: 16 (over y_hi, z, core).
Axes of the slice: x: 4, y: 4 (y_hi: 2, y_lo: 2; y = y_hi * 2 + y_lo), z: 4, core: 2. Of those that a mesh axis runs over, the one named last changes fastest.
Arguments:
- left_act: bfloat16 [512, 512, 32], P(None, ('row', 'col')), may hold values from -24 to 24
- right_act: bfloat16 [512, 512, 32], P('row', 'col'), may hold values from -24 to 24
- proj_weight: bfloat16 [1024, 128], replicated, may hold values from -0.1875 to 0.1875
- proj_bias: float32 [128], replicated, may hold values from -6 to 6
Outputs:
- pair_update: float32 [512, 512, 128], P('row', 'col')
The draws below stay inside these ranges and needn't reach their ends.
All inputs are finite; a program needn't handle non-finite values.
Results may differ from the reference program's by a relative error of at most 0.0016.
Values may be sent and summed in bfloat16 or wider, within the bound.
A program may use at most 64 MiB of HBM per device.

```python
import jax
import jax.numpy as jnp
from jax import lax

C = 32
CP = 128
S = 512
R = 512


def block_scale(key, extent, split, low, top_value):
    loudness, own = 1.0, jax.random.fold_in(key, 6)
    for position, parts in split:
        heights = jnp.exp(jax.random.uniform(jax.random.fold_in(own, position), (parts,), jnp.float32, low / len(split), top_value / len(split)))
        loudness = loudness * jnp.repeat(heights, extent[position] // parts).reshape([-1 if axis == position else 1 for axis in range(len(extent))])
    return loudness


def normal_values(key, shape, deviation, reach, pieces=(), kind=jnp.bfloat16):
    entries = deviation * jax.random.normal(key, shape, jnp.float32)
    if pieces:
        entries = entries * block_scale(key, shape, pieces, -0.22, 0.18)
    return jnp.clip(entries, -reach, reach).astype(kind)


def setup_inputs(seed: int = 0) -> dict:
    arg_keys = jax.random.split(jax.random.key(seed), 5)
    return {
        "left_act": normal_values(arg_keys[0], (S, R, C), 4.0, 24.0, ((1, 128),)),
        "right_act": normal_values(arg_keys[1], (S, R, C), 4.0, 24.0, ((0, 8), (1, 16))),
        "proj_weight": normal_values(arg_keys[2], (C * C, CP), (C * C) ** -0.5, 0.1875),
        "proj_bias": normal_values(arg_keys[3], (CP,), 1.0, 6.0, (), jnp.float32),
    }


def reference(left_act, right_act, proj_weight, proj_bias):
    right_wide = right_act.astype(jnp.float32)
    weight_three = proj_weight.astype(jnp.float32).reshape(C, C, CP)
    block_rows = 8

    def one_block(index_block):
        left_block = lax.dynamic_slice_in_dim(left_act, index_block * block_rows, block_rows, 1).astype(jnp.float32)
        outer_sum = jnp.einsum("sic,sje->icje", left_block, right_wide)
        outer_mean = (outer_sum / S).astype(jnp.bfloat16)
        tile_out = jnp.einsum("icje,cef->ijf", outer_mean.astype(jnp.float32), weight_three)
        return tile_out + proj_bias

    blocks = lax.map(one_block, jnp.arange(R // block_rows, dtype=jnp.int32))
    return blocks.reshape(R, R, CP)
```

```python
import jax
import jax.numpy as jnp
from jax import lax
from jax.experimental import pallas as pl
from jax.experimental.pallas import tpu as pltpu
from jax.sharding import PartitionSpec as P

C, CP, S = 32, 128, 512
MESH = pl.DeviceIdType.MESH
COMPUTE = True
COMM = True


def chunk_exchange(slabs, lane):
    a0, a1, a2, a3 = slabs
    low = lane < 64

    def swap64(a, b):
        return jnp.where(low, a, pltpu.roll(b, 64, 1)), jnp.where(low, pltpu.roll(a, 64, 1), b)

    def swap32(a, b):
        even = (lane % 64) < 32
        return jnp.where(even, a, pltpu.roll(b, 32, 1)), jnp.where(even, pltpu.roll(a, 96, 1), b)

    b0, b2 = swap64(a0, a2)
    b1, b3 = swap64(a1, a3)
    c0, c1 = swap32(b0, b1)
    c2, c3 = swap32(b2, b3)
    return c0, c1, c2, c3


def kernel(lt_hbm, rt_hbm, w_hbm, bias_ref, out_ref,
           lg, rp, rall, rt_v, w_v, wp, wide, pbuf,
           local_sems, ls, lr, rs, rr):
    row, col = lax.axis_index("row"), lax.axis_index("col")
    x, yl = row // 2, row % 2
    yh, z, c = col // 8, (col // 2) % 4, col % 2

    def dev(dx=0, dyl=0, dyh=0, dz=0, dc=0):
        xx, zz = (x + dx + 4) % 4, (z + dz + 4) % 4
        yyl = 1 - yl if dyl else yl
        yyh = 1 - yh if dyh else yh
        cc = 1 - c if dc else c
        return (xx * 2 + yyl, (yyh * 4 + zz) * 2 + cc)

    def lslot(dyh=0, dz=0, dc=0):
        q = dev(dyh=dyh, dz=dz, dc=dc)[1]
        return lg.at[pl.ds(pl.multiple_of(q * 128, 128), 128), :]

    def rslot(dx=0, dyl=0):
        r = dev(dx=dx, dyl=dyl)[0]
        return rp.at[pl.ds(pl.multiple_of(r * 512, 512), 512), :]

    load_l = pltpu.make_async_copy(lt_hbm, lslot(), local_sems.at[0])
    load_r = pltpu.make_async_copy(rt_hbm, rt_v, local_sems.at[1])
    load_w = pltpu.make_async_copy(w_hbm, w_v, local_sems.at[2])
    load_r.start()
    load_l.start()
    load_w.start()

    barrier = pltpu.get_barrier_semaphore()
    peers = [dev(dx=1), dev(dx=-1), dev(dyl=1), dev(dyh=1), dev(dz=1), dev(dz=-1), dev(dc=1)]
    for peer in peers:
        pl.semaphore_signal(barrier, inc=1, device_id=peer, device_id_type=MESH)

    lane_f = lax.broadcasted_iota(jnp.int32, (32, 128), 1)
    load_r.wait()
    wide[:, 0:64] = rt_v[...].astype(jnp.float32)
    own_r = rslot()
    for e in range(16):
        lo = wide[pl.ds(e, 32, stride=32), :]
        hi = wide[pl.ds(e + 16, 32, stride=32), :]
        both = jnp.where(lane_f < 64, lo, pltpu.roll(hi, 64, 1))
        own_r[pl.ds(e * 32, 32), :] = both.astype(jnp.bfloat16)
    load_l.wait()

    pl.semaphore_wait(barrier, len(peers))

    def lcopy(slot, to, k):
        return pltpu.make_async_remote_copy(
            src_ref=slot, dst_ref=slot, send_sem=ls.at[k], recv_sem=lr.at[k],
            device_id=to, device_id_type=MESH)

    def rcopy(slot, to, k):
        return pltpu.make_async_remote_copy(
            src_ref=slot, dst_ref=slot, send_sem=rs.at[k], recv_sem=rr.at[k],
            device_id=to, device_id_type=MESH)

    up, down, pair, sib = dev(dz=1), dev(dz=-1), dev(dyh=1), dev(dc=1)
    xup, xdown, ypair = dev(dx=1), dev(dx=-1), dev(dyl=1)
    if COMM:
        r_pair = rcopy(rslot(), ypair, 0)
        r_up, r_down = rcopy(rslot(), xup, 1), rcopy(rslot(), xdown, 2)
        l_pair = lcopy(lslot(), pair, 0)
        l_up, l_down = lcopy(lslot(), up, 1), lcopy(lslot(), down, 2)
        l_sib = lcopy(lslot(), sib, 7)
        for t in (r_pair, l_pair, r_up, r_down, l_up, l_down, l_sib):
            t.start()
        r_pair.wait_recv()
        r_pup, r_pdown = rcopy(rslot(dyl=1), xup, 3), rcopy(rslot(dyl=1), xdown, 4)
        r_pup.start()
        r_pdown.start()
        l_pair.wait_recv()
        l_pup, l_pdown = lcopy(lslot(dyh=1), up, 3), lcopy(lslot(dyh=1), down, 4)
        s_pair = lcopy(lslot(dyh=1), sib, 8)
        for t in (l_pup, l_pdown, s_pair):
            t.start()
        r_down.wait_recv()
        r_rel = rcopy(rslot(dx=1), xdown, 5)
        r_rel.start()
        l_down.wait_recv()
        l_rel = lcopy(lslot(dz=1), down, 5)
        s_a = lcopy(lslot(dz=1), sib, 9)
        l_rel.start()
        s_a.start()
        l_up.wait_recv()
        s_b = lcopy(lslot(dz=-1), sib, 10)
        s_b.start()
        r_up.wait_recv()
        r_pup.wait_recv()
        r_prel = rcopy(rslot(dx=-1, dyl=1), xup, 6)
        r_prel.start()
        l_pup.wait_recv()
        l_prel = lcopy(lslot(dyh=1, dz=-1), up, 6)
        s_c = lcopy(lslot(dyh=1, dz=-1), sib, 11)
        l_prel.start()
        s_c.start()
        l_pdown.wait_recv()
        s_d = lcopy(lslot(dyh=1, dz=1), sib, 12)
        s_d.start()
        l_rel.wait_recv()
        s_e = lcopy(lslot(dz=2), sib, 13)
        s_e.start()
        l_prel.wait_recv()
        s_f = lcopy(lslot(dyh=1, dz=2), sib, 14)
        s_f.start()
        for t in (r_pdown, r_rel, r_prel, l_sib, s_pair, s_a, s_b, s_c, s_d, s_e, s_f):
            t.wait_recv()
        for t in (r_pair, r_up, r_down, r_pup, r_pdown, r_rel, r_prel,
                  l_pair, l_up, l_down, l_sib, l_pup, l_pdown, l_rel, l_prel,
                  s_pair, s_a, s_b, s_c, s_d, s_e, s_f):
            t.wait_send()

    load_w.wait()
    if not COMPUTE:
        out_ref[...] = jnp.zeros_like(out_ref)
        return
    wide[...] = w_v[...].astype(jnp.float32)
    for e in range(32):
        wp[pl.ds(e * 32, 32), :] = wide[pl.ds(e, 32, stride=32), :].astype(jnp.bfloat16)

    lane = lax.broadcasted_iota(jnp.int32, (512, 128), 1)
    for xx in range(4):
        a = rp[xx * 1024:xx * 1024 + 512, :]
        b = rp[xx * 1024 + 512:xx * 1024 + 1024, :]
        rall[0:512, xx * 128:xx * 128 + 128] = jnp.where(lane < 64, a, pltpu.roll(b, 64, 1))
        rall[512:1024, xx * 128:xx * 128 + 128] = jnp.where(lane < 64, pltpu.roll(a, 64, 1), b)

    lane_s = lax.broadcasted_iota(jnp.int32, (32, 128), 1)

    def pair_step(p, carry):
        lblock = lg[pl.ds(pl.multiple_of(p * 256, 256), 256), :]
        for g in range(8):
            o = lax.dot_general(rall[g * 128:g * 128 + 128, :], lblock, (((1,), (1,)), ((), ())),
                                preferred_element_type=jnp.float32).astype(jnp.bfloat16)
            for h in range(2):
                slabs = [o[k * 32:k * 32 + 32, h * 128:h * 128 + 128] for k in range(4)]
                for i, t in enumerate(chunk_exchange(slabs, lane_s)):
                    pbuf[h * 128 + i * 32:h * 128 + i * 32 + 32, g * 128:g * 128 + 128] = t
        tile = jnp.dot(pbuf[...], wp[...], preferred_element_type=jnp.float32)
        out_ref[pl.ds(pl.multiple_of(p * 256, 256), 256), :] = tile * (1.0 / S) + bias_ref[...]
        return carry

    lax.fori_loop(0, 8, pair_step, 0)


def on_device(left_act, right_act, proj_weight, proj_bias):
    lt = jnp.transpose(left_act, (1, 2, 0)).reshape(128, S)
    rt = jnp.transpose(right_act, (1, 2, 0)).reshape(1024, 64)
    hbm, vmem = pl.BlockSpec(memory_space=pl.ANY), pl.BlockSpec(memory_space=pltpu.VMEM)
    out = pl.pallas_call(
        kernel,
        out_shape=jax.ShapeDtypeStruct((2048, CP), jnp.float32),
        in_specs=[hbm, hbm, hbm, vmem],
        out_specs=vmem,
        scratch_shapes=[
            pltpu.VMEM((2048, S), jnp.bfloat16),
            pltpu.VMEM((4096, 128), jnp.bfloat16),
            pltpu.VMEM((1024, S), jnp.bfloat16),
            pltpu.VMEM((1024, 64), jnp.bfloat16),
            pltpu.VMEM((1024, 128), jnp.bfloat16),
            pltpu.VMEM((1024, 128), jnp.bfloat16),
            pltpu.VMEM((1024, 128), jnp.float32),
            pltpu.VMEM((256, 1024), jnp.bfloat16),
            pltpu.SemaphoreType.DMA((3,)),
            pltpu.SemaphoreType.DMA((15,)),
            pltpu.SemaphoreType.DMA((15,)),
            pltpu.SemaphoreType.DMA((7,)),
            pltpu.SemaphoreType.DMA((7,)),
        ],
        compiler_params=pltpu.CompilerParams(
            collective_id=0, has_side_effects=True, vmem_limit_bytes=32 * 1024 * 1024
        ),
        cost_estimate=pl.CostEstimate(flops=2684354560, bytes_accessed=4 << 20, transcendentals=0),
    )(lt, rt, proj_weight, proj_bias.reshape(1, CP))
    return out.reshape(64, 32, CP)


def solution(mesh):
    return jax.shard_map(
        on_device,
        mesh=mesh,
        in_specs=(P(None, ("row", "col"), None), P("row", "col", None), P(), P()),
        out_specs=P("row", "col", None),
        check_vma=False,
    )
```

```python
import jax
import jax.numpy as jnp
from jax import lax
from jax.experimental import pallas as pl
from jax.experimental.pallas import tpu as pltpu
from jax.sharding import PartitionSpec as P

C, CP, S = 32, 128, 512
MESH = pl.DeviceIdType.MESH
NC = 2
NT = (((1,), (1,)), ((), ()))


def ranged(start, size):
    return pl.ds(pl.multiple_of(start, size), size)


def swap_halves(block):
    count = block.shape[0] // 64
    return jnp.concatenate([block[64 * (k ^ 1):64 * (k ^ 1) + 64] for k in range(count)], axis=0)


def product(a, b):
    return lax.dot_general(a, b, NT, preferred_element_type=jnp.float32)


def kernel(lt_hbm, rt_hbm, w_hbm, bias_hbm, out_ref,
           lg, rp, rall, lt_v, rt_v, w_v, bias_v, wp, wide, pb, wb, acc,
           local_sems, ls, lr, rs, rr, ss, sr):
    row, col = lax.axis_index("row"), lax.axis_index("col")
    x, yl = row // 2, row % 2
    yh, z, c = col // 8, (col // 2) % 4, col % 2

    def dev(dx=0, dyl=0, dyh=0, dz=0, dc=0):
        xx, zz = (x + dx + 4) % 4, (z + dz + 4) % 4
        yyl = 1 - yl if dyl else yl
        yyh = 1 - yh if dyh else yh
        cc = 1 - c if dc else c
        return (xx * 2 + yyl, (yyh * 4 + zz) * 2 + cc)

    def slot(kind, p=0, d=0, part=None):
        size = 128 if kind == "l" else 512
        index = dev(dyh=p, dz=d)[1] if kind == "l" else dev(dyl=p, dx=d)[0]
        buffer = lg if kind == "l" else rp
        if part is None:
            return buffer.at[ranged(index * size, size), :]
        piece = size // NC
        return buffer.at[ranged(index * size + part * piece, piece), :]

    load_l = pltpu.make_async_copy(lt_hbm, lt_v, local_sems.at[0])
    load_r = pltpu.make_async_copy(rt_hbm, rt_v, local_sems.at[1])
    load_w = pltpu.make_async_copy(w_hbm, w_v, local_sems.at[2])
    load_b = pltpu.make_async_copy(bias_hbm, bias_v, local_sems.at[3])
    for load in (load_l, load_r, load_w, load_b):
        load.start()

    barrier = pltpu.get_barrier_semaphore()
    peers = [dev(dx=1), dev(dx=-1), dev(dx=2), dev(dyl=1), dev(dyh=1),
             dev(dz=1), dev(dz=-1), dev(dz=2), dev(dc=1)]
    for peer in peers:
        pl.semaphore_signal(barrier, inc=1, device_id=peer, device_id_type=MESH)

    def interleave(a, b):
        low = lax.broadcasted_iota(jnp.int32, a.shape, 1) < 64
        return jnp.where(low, a, pltpu.roll(b, 64, 1)), jnp.where(low, pltpu.roll(a, 64, 1), b)

    load_l.wait()
    own_l = ranged(col * 128, 128)
    for t in range(2):
        even, odd = interleave(lt_v[:, t * 256:t * 256 + 128], lt_v[:, t * 256 + 128:t * 256 + 256])
        lg[own_l, t * 128:t * 128 + 128] = even
        lg[own_l, 256 + t * 128:256 + t * 128 + 128] = odd
    lane_f = lax.broadcasted_iota(jnp.int32, (32, 128), 1)

    def prepare_right():
        load_r.wait()
        wide[:, 0:64] = rt_v[...].astype(jnp.float32)
        for e in range(16):
            lo = wide[pl.ds(e, 32, stride=32), :]
            hi = wide[pl.ds(e + 16, 32, stride=32), :]
            both = jnp.where(lane_f < 64, lo, pltpu.roll(hi, 64, 1))
            rp[ranged(row * 512 + e * 32, 32), :] = both.astype(jnp.bfloat16)

    def prepare_weight():
        load_w.wait()
        load_b.wait()
        wide[...] = w_v[...].astype(jnp.float32)
        for e in range(32):
            wp[pl.ds(e * 32, 32), :] = wide[pl.ds(e, 32, stride=32), :].astype(jnp.bfloat16)
        zero = jnp.zeros((32, 128), jnp.bfloat16)
        for side in range(2):
            for e in range(16):
                for h in range(2):
                    source = (e + 16 * (h ^ side)) * 32
                    block = wp[source:source + 32, :]
                    for i2 in range(2):
                        r = side * 2048 + e * 128 + h * 64 + i2 * 32
                        wb[r:r + 32, i2 * 128:i2 * 128 + 128] = block
                        wb[r:r + 32, (1 - i2) * 128:(1 - i2) * 128 + 128] = zero

    def mover(send, recv):
        started = []

        def move(ref, to):
            k = len(started)
            copy = pltpu.make_async_remote_copy(
                src_ref=ref, dst_ref=ref, send_sem=send.at[k], recv_sem=recv.at[k],
                device_id=to, device_id_type=MESH)
            copy.start()
            started.append(copy)
            return copy
        return move, started

    lmove, lsent = mover(ls, lr)
    rmove, rsent = mover(rs, rr)
    smove, ssent = mover(ss, sr)
    move = {"l": lmove, "r": rmove}
    to = {"l": {"up": dev(dz=1), "down": dev(dz=-1), "far": dev(dz=2), "pair": dev(dyh=1)},
          "r": {"up": dev(dx=1), "down": dev(dx=-1), "far": dev(dx=2), "pair": dev(dyl=1)}}
    sib = dev(dc=1)
    parts = range(NC)
    ways = ("far", "up", "down")
    came = {"up": -1, "down": 1, "far": 2}
    g = {}
    sibs = {}

    def share(p, d):
        sibs[p, d] = smove(slot("l", p, d), sib)

    def send_pair(kind, k):
        g[kind, "pair", k] = move[kind](slot(kind, 0, 0, k), to[kind]["pair"])

    def send_own(kind, way):
        g[kind, way, 0] = move[kind](slot(kind), to[kind][way])

    def send_on(kind, k):
        g[kind, "pair", k].wait_recv()
        for way in ways:
            g[kind, way, 1, k] = move[kind](slot(kind, 1, 0, k), to[kind][way])

    prepare_right()
    pl.semaphore_wait(barrier, len(peers))
    for k in parts:
        send_pair("l", k)
        send_pair("r", k)
    for way in ("up", "down", "far"):
        send_own("l", way)
        send_own("r", way)
    share(0, 0)
    prepare_weight()

    def unpack(m):
        parity = yl if m == 0 else 1 - yl
        for t in range(2):
            a = rp[ranged((4 * t + parity) * 512, 512), :]
            b = rp[ranged((4 * t + 2 + parity) * 512, 512), :]
            low, high = interleave(a, b)
            rall[0:512, m * 256 + t * 128:m * 256 + t * 128 + 128] = low
            rall[512:1024, m * 256 + t * 128:m * 256 + t * 128 + 128] = high

    lanes = [ranged(yl * 256, 256), ranged((1 - yl) * 256, 256)]
    lowlane = lax.broadcasted_iota(jnp.int32, (512, 256), 1) % 128 < 64

    def mix(o_lo, o_hi, rows):
        o_lo, o_hi = o_lo.astype(jnp.bfloat16), o_hi.astype(jnp.bfloat16)
        for side, mixed in enumerate((jnp.where(lowlane, o_lo, o_hi), jnp.where(lowlane, o_hi, o_lo))):
            for e in range(16):
                for t, r in enumerate(rows):
                    pb[side, r:r + 32, e * 128:e * 128 + 128] = mixed[e * 32:e * 32 + 32, t * 128:t * 128 + 128]

    def project(first, blocks):
        count = 32 * len(blocks)
        for side in range(2):
            res = jnp.dot(pb[side, first:first + count, :], wb[side * 2048:side * 2048 + 2048, :],
                          preferred_element_type=jnp.float32)
            for t, b in enumerate(blocks):
                for i2 in range(2):
                    out_ref[ranged(b * 128 + (2 * side + i2) * 32, 32), :] = (
                        res[t * 32:t * 32 + 32, i2 * 128:i2 * 128 + 128] * (1.0 / S) + bias_v[...])

    for k in parts:
        send_on("l", k)
        send_on("r", k)
    share(1, 0)
    for way in ways:
        g["l", way, 0].wait_recv()
        share(0, came[way])
        g["r", way, 0].wait_recv()
    for p, d in ((0, 0), (0, 2), (0, -1), (0, 1)):
        sibs[p, d].wait_recv()
    unpack(0)
    for t in range(4):
        block = lg[ranged(yh * 1024 + t * 256, 256), lanes[0]]
        acc[2 * t] = product(rall[0:512, 0:256], block)
        acc[2 * t + 1] = product(rall[512:1024, 0:256], swap_halves(block))

    for way in ways:
        for k in parts:
            g["l", way, 1, k].wait_recv()
        share(1, came[way])
        for k in parts:
            g["r", way, 1, k].wait_recv()
    unpack(1)
    for t in range(4):
        block = lg[ranged(yh * 1024 + t * 256, 256), lanes[1]]
        mix(acc[2 * t] + product(rall[0:512, 256:512], block),
            acc[2 * t + 1] + product(rall[512:1024, 256:512], swap_halves(block)),
            (t * 64, t * 64 + 32))
    project(0, [yh * 8 + t for t in range(8)])

    other = (1 - yh) * 8
    for who in range(2):
        core = c if who == 0 else 1 - c
        if who == 1:
            for d in (0, 2, -1, 1):
                sibs[1, d].wait_recv()
        for t in range(2):
            block = jnp.concatenate(
                [jnp.concatenate([lg[ranged((other + (2 * t + u) * 2 + core) * 128, 128), lanes[m]] for m in range(2)], axis=1)
                 for u in range(2)], axis=0)
            r = 256 + who * 128 + t * 64
            mix(product(rall[0:512, :], block), product(rall[512:1024, :], swap_halves(block)), (r, r + 32))
    project(256, [other + t * 2 + (c if who == 0 else 1 - c) for who in range(2) for t in range(4)])
    for copy in lsent + rsent + ssent:
        copy.wait_send()


def on_device(left_act, right_act, proj_weight, proj_bias):
    lt = jnp.transpose(left_act, (1, 2, 0)).reshape(128, S)
    rt = jnp.transpose(right_act, (1, 2, 0)).reshape(1024, 64)
    bias = proj_bias.reshape(1, CP)
    hbm, vmem = pl.BlockSpec(memory_space=pltpu.HBM), pl.BlockSpec(memory_space=pltpu.VMEM)
    dma = pltpu.SemaphoreType.DMA
    arrays = [pltpu.with_memory_space_constraint(a, pltpu.HBM) for a in (lt, rt, proj_weight, bias)]
    out = pl.pallas_call(
        kernel,
        out_shape=jax.ShapeDtypeStruct((2048, CP), jnp.float32),
        in_specs=[hbm, hbm, hbm, hbm],
        out_specs=vmem,
        scratch_shapes=[
            pltpu.VMEM((2048, S), jnp.bfloat16),
            pltpu.VMEM((4096, 128), jnp.bfloat16),
            pltpu.VMEM((1024, S), jnp.bfloat16),
            pltpu.VMEM((128, S), jnp.bfloat16),
            pltpu.VMEM((1024, 64), jnp.bfloat16),
            pltpu.VMEM((1024, 128), jnp.bfloat16),
            pltpu.VMEM((1, 128), jnp.float32),
            pltpu.VMEM((1024, 128), jnp.bfloat16),
            pltpu.VMEM((1024, 128), jnp.float32),
            pltpu.VMEM((2, 512, 2048), jnp.bfloat16),
            pltpu.VMEM((4096, 256), jnp.bfloat16),
            pltpu.VMEM((8, 512, 256), jnp.float32),
            dma((4,)), dma((16,)), dma((16,)), dma((16,)), dma((16,)), dma((8,)), dma((8,)),
        ],
        compiler_params=pltpu.CompilerParams(
            collective_id=0, has_side_effects=True, vmem_limit_bytes=40 * 1024 * 1024
        ),
        cost_estimate=pl.CostEstimate(flops=3221225472, bytes_accessed=4 << 20, transcendentals=0),
    )(*arrays)
    return out.reshape(64, 32, CP)


def solution(mesh):
    return jax.shard_map(
        on_device,
        mesh=mesh,
        in_specs=(P(None, ("row", "col"), None), P("row", "col", None), P(), P()),
        out_specs=P("row", "col", None),
        check_vma=False,
    )
```

```python
import jax
import jax.numpy as jnp
from jax import lax
from jax.experimental import pallas as pl
from jax.experimental.pallas import tpu as pltpu
from jax.sharding import PartitionSpec as P

C, CP, S = 32, 128, 512
MESH = pl.DeviceIdType.MESH
PARTS = {"l": ((0, 3), (3, 5)), "r": ((0, 3), (3, 5))}
AROUND = {"l": (1,), "r": (1,)}
NT = (((1,), (1,)), ((), ()))


def ranged(start, size):
    return pl.ds(pl.multiple_of(start, size), size)


def swap_halves(block):
    count = block.shape[0] // 64
    return jnp.concatenate([block[64 * (k ^ 1):64 * (k ^ 1) + 64] for k in range(count)], axis=0)


def product(a, b):
    return lax.dot_general(a, b, NT, preferred_element_type=jnp.float32)


def kernel(lt_hbm, rt_hbm, w_hbm, bias_hbm, out_ref,
           lg, rp, rall, lt_v, rt_v, w_v, bias_v, wp, wide, pb, wb, acc,
           local_sems, ls, lr, rs, rr, ss, sr):
    row, col = lax.axis_index("row"), lax.axis_index("col")
    x, yl = row // 2, row % 2
    yh, z, c = col // 8, (col // 2) % 4, col % 2

    def dev(dx=0, dyl=0, dyh=0, dz=0, dc=0):
        xx, zz = (x + dx + 4) % 4, (z + dz + 4) % 4
        yyl = 1 - yl if dyl else yl
        yyh = 1 - yh if dyh else yh
        cc = 1 - c if dc else c
        return (xx * 2 + yyl, (yyh * 4 + zz) * 2 + cc)

    def slot(kind, p=0, d=0, part=None):
        size = 128 if kind == "l" else 512
        index = dev(dyh=p, dz=d)[1] if kind == "l" else dev(dyl=p, dx=d)[0]
        buffer = lg if kind == "l" else rp
        if part is None:
            return buffer.at[ranged(index * size, size), :]
        first, count = PARTS[kind][part]
        step = size // 8
        return buffer.at[pl.ds(pl.multiple_of(index * size + first * step, step), count * step), :]

    load_l = pltpu.make_async_copy(lt_hbm, lt_v, local_sems.at[0])
    load_r = pltpu.make_async_copy(rt_hbm, rt_v, local_sems.at[1])
    load_w = pltpu.make_async_copy(w_hbm, w_v, local_sems.at[2])
    load_b = pltpu.make_async_copy(bias_hbm, bias_v, local_sems.at[3])
    for load in (load_l, load_r, load_w, load_b):
        load.start()

    barrier = pltpu.get_barrier_semaphore()
    peers = [dev(dx=1), dev(dx=-1), dev(dx=2), dev(dyl=1), dev(dyh=1),
             dev(dz=1), dev(dz=-1), dev(dz=2), dev(dc=1)]
    for peer in peers:
        pl.semaphore_signal(barrier, inc=1, device_id=peer, device_id_type=MESH)

    def interleave(a, b):
        low = lax.broadcasted_iota(jnp.int32, a.shape, 1) < 64
        return jnp.where(low, a, pltpu.roll(b, 64, 1)), jnp.where(low, pltpu.roll(a, 64, 1), b)

    load_l.wait()
    own_l = ranged(col * 128, 128)
    for t in range(2):
        even, odd = interleave(lt_v[:, t * 256:t * 256 + 128], lt_v[:, t * 256 + 128:t * 256 + 256])
        lg[own_l, t * 128:t * 128 + 128] = even
        lg[own_l, 256 + t * 128:256 + t * 128 + 128] = odd
    lane_f = lax.broadcasted_iota(jnp.int32, (32, 128), 1)

    def prepare_right():
        load_r.wait()
        wide[:, 0:64] = rt_v[...].astype(jnp.float32)
        for e in range(16):
            lo = wide[pl.ds(e, 32, stride=32), :]
            hi = wide[pl.ds(e + 16, 32, stride=32), :]
            both = jnp.where(lane_f < 64, lo, pltpu.roll(hi, 64, 1))
            rp[ranged(row * 512 + e * 32, 32), :] = both.astype(jnp.bfloat16)

    def prepare_weight():
        load_w.wait()
        load_b.wait()
        wide[...] = w_v[...].astype(jnp.float32)
        for e in range(32):
            wp[pl.ds(e * 32, 32), :] = wide[pl.ds(e, 32, stride=32), :].astype(jnp.bfloat16)
        zero = jnp.zeros((32, 128), jnp.bfloat16)
        for side in range(2):
            for e in range(16):
                for h in range(2):
                    source = (e + 16 * (h ^ side)) * 32
                    block = wp[source:source + 32, :]
                    for i2 in range(2):
                        r = side * 2048 + e * 128 + h * 64 + i2 * 32
                        wb[r:r + 32, i2 * 128:i2 * 128 + 128] = block
                        wb[r:r + 32, (1 - i2) * 128:(1 - i2) * 128 + 128] = zero

    def mover(send, recv):
        started = []

        def move(ref, to):
            k = len(started)
            copy = pltpu.make_async_remote_copy(
                src_ref=ref, dst_ref=ref, send_sem=send.at[k], recv_sem=recv.at[k],
                device_id=to, device_id_type=MESH)
            copy.start()
            started.append(copy)
            return copy
        return move, started

    lmove, lsent = mover(ls, lr)
    rmove, rsent = mover(rs, rr)
    smove, ssent = mover(ss, sr)
    move = {"l": lmove, "r": rmove}
    to = {"l": {"up": dev(dz=1), "down": dev(dz=-1), "far": dev(dz=2), "pair": dev(dyh=1)},
          "r": {"up": dev(dx=1), "down": dev(dx=-1), "far": dev(dx=2), "pair": dev(dyl=1)}}
    sib = dev(dc=1)
    parts = {kind: range(len(PARTS[kind])) for kind in PARTS}
    most = range(max(len(parts["l"]), len(parts["r"])))
    ways = ("far", "up", "down")
    came = {"up": -1, "down": 1, "far": 2}
    g = {}
    sibs = {}

    def share(p, d, k=None):
        sibs[p, d, k] = smove(slot("l", p, d, k), sib)

    def send_pair(kind, k):
        g[kind, "pair", k] = move[kind](slot(kind, 0, 0, k), to[kind]["pair"])

    def send_own(kind, way, k=None):
        key = (kind, way, 0) if k is None else (kind, way, 0, k)
        g[key] = move[kind](slot(kind, 0, 0, k), to[kind][way])

    def send_on(kind, k):
        g[kind, "pair", k].wait_recv()
        for way in ways:
            if way != "far" or k not in AROUND[kind]:
                g[kind, way, 1, k] = move[kind](slot(kind, 1, 0, k), to[kind][way])

    def send_around(kind, k):
        g[kind, "far", 0, k].wait_recv()
        g[kind, "far", 1, k] = move[kind](slot(kind, 0, 2, k), to[kind]["pair"])

    prepare_right()
    pl.semaphore_wait(barrier, len(peers))
    for kind in ("l", "r"):
        for k in parts[kind]:
            send_pair(kind, k)
    for kind in ("l", "r"):
        for k in sorted(parts[kind], key=lambda k: k not in AROUND[kind]):
            send_own(kind, "far", k)
    for way in ("up", "down"):
        send_own("l", way)
        send_own("r", way)
    share(0, 0)
    prepare_weight()

    def unpack(m):
        parity = yl if m == 0 else 1 - yl
        for t in range(2):
            a = rp[ranged((4 * t + parity) * 512, 512), :]
            b = rp[ranged((4 * t + 2 + parity) * 512, 512), :]
            low, high = interleave(a, b)
            rall[0:512, m * 256 + t * 128:m * 256 + t * 128 + 128] = low
            rall[512:1024, m * 256 + t * 128:m * 256 + t * 128 + 128] = high

    lanes = [ranged(yl * 256, 256), ranged((1 - yl) * 256, 256)]
    lowlane = lax.broadcasted_iota(jnp.int32, (512, 256), 1) % 128 < 64

    def mix(o_lo, o_hi, rows):
        o_lo, o_hi = o_lo.astype(jnp.bfloat16), o_hi.astype(jnp.bfloat16)
        for side, mixed in enumerate((jnp.where(lowlane, o_lo, o_hi), jnp.where(lowlane, o_hi, o_lo))):
            for e in range(16):
                for t, r in enumerate(rows):
                    pb[side, r:r + 32, e * 128:e * 128 + 128] = mixed[e * 32:e * 32 + 32, t * 128:t * 128 + 128]

    def project(first, blocks):
        count = 32 * len(blocks)
        for side in range(2):
            res = jnp.dot(pb[side, first:first + count, :], wb[side * 2048:side * 2048 + 2048, :],
                          preferred_element_type=jnp.float32)
            for t, b in enumerate(blocks):
                for i2 in range(2):
                    out_ref[ranged(b * 128 + (2 * side + i2) * 32, 32), :] = (
                        res[t * 32:t * 32 + 32, i2 * 128:i2 * 128 + 128] * (1.0 / S) + bias_v[...])

    for k in most:
        for kind in ("l", "r"):
            if k in parts[kind]:
                send_on(kind, k)
    for kind in ("l", "r"):
        for k in AROUND[kind]:
            send_around(kind, k)
    share(1, 0)
    for way in ways:
        for kind in ("l", "r"):
            if way == "far":
                for k in parts[kind]:
                    if k not in AROUND[kind]:
                        g[kind, way, 0, k].wait_recv()
            else:
                g[kind, way, 0].wait_recv()
            if kind == "l":
                share(0, came[way])
    for d in (0, 2, -1, 1):
        sibs[0, d, None].wait_recv()
    unpack(0)
    for t in range(4):
        block = lg[ranged(yh * 1024 + t * 256, 256), lanes[0]]
        acc[2 * t] = product(rall[0:512, 0:256], block)
        acc[2 * t + 1] = product(rall[512:1024, 0:256], swap_halves(block))

    def pass_on(k):
        for way in ways:
            g["l", way, 1, k].wait_recv()
            share(1, came[way], k)

    def finish(t):
        block = lg[ranged(yh * 1024 + t * 256, 256), lanes[1]]
        mix(acc[2 * t] + product(rall[0:512, 256:512], block),
            acc[2 * t + 1] + product(rall[512:1024, 256:512], swap_halves(block)),
            (t * 64, t * 64 + 32))

    for k in parts["l"]:
        pass_on(k)
    for k in parts["r"]:
        for way in ways:
            g["r", way, 1, k].wait_recv()
    unpack(1)
    for t in range(0):
        finish(t)
    for t in range(0, 4):
        finish(t)
    project(0, [yh * 8 + t for t in range(8)])

    other = (1 - yh) * 8
    for who in range(2):
        core = c if who == 0 else 1 - c
        if who == 1:
            sibs[1, 0, None].wait_recv()
            for k in parts["l"]:
                for d in (2, -1, 1):
                    sibs[1, d, k].wait_recv()
        for t in range(2):
            block = jnp.concatenate(
                [jnp.concatenate([lg[ranged((other + (2 * t + u) * 2 + core) * 128, 128), lanes[m]] for m in range(2)], axis=1)
                 for u in range(2)], axis=0)
            r = 256 + who * 128 + t * 64
            mix(product(rall[0:512, :], block), product(rall[512:1024, :], swap_halves(block)), (r, r + 32))
    project(256, [other + t * 2 + (c if who == 0 else 1 - c) for who in range(2) for t in range(4)])
    for copy in lsent + rsent + ssent:
        copy.wait_send()


def on_device(left_act, right_act, proj_weight, proj_bias):
    lt = jnp.transpose(left_act, (1, 2, 0)).reshape(128, S)
    rt = jnp.transpose(right_act, (1, 2, 0)).reshape(1024, 64)
    bias = proj_bias.reshape(1, CP)
    hbm, vmem = pl.BlockSpec(memory_space=pltpu.HBM), pl.BlockSpec(memory_space=pltpu.VMEM)
    dma = pltpu.SemaphoreType.DMA
    arrays = [pltpu.with_memory_space_constraint(a, pltpu.HBM) for a in (lt, rt, proj_weight, bias)]
    out = pl.pallas_call(
        kernel,
        out_shape=jax.ShapeDtypeStruct((2048, CP), jnp.float32),
        in_specs=[hbm, hbm, hbm, hbm],
        out_specs=vmem,
        scratch_shapes=[
            pltpu.VMEM((2048, S), jnp.bfloat16),
            pltpu.VMEM((4096, 128), jnp.bfloat16),
            pltpu.VMEM((1024, S), jnp.bfloat16),
            pltpu.VMEM((128, S), jnp.bfloat16),
            pltpu.VMEM((1024, 64), jnp.bfloat16),
            pltpu.VMEM((1024, 128), jnp.bfloat16),
            pltpu.VMEM((1, 128), jnp.float32),
            pltpu.VMEM((1024, 128), jnp.bfloat16),
            pltpu.VMEM((1024, 128), jnp.float32),
            pltpu.VMEM((2, 512, 2048), jnp.bfloat16),
            pltpu.VMEM((4096, 256), jnp.bfloat16),
            pltpu.VMEM((8, 512, 256), jnp.float32),
            dma((4,)), dma((20,)), dma((20,)), dma((20,)), dma((20,)), dma((20,)), dma((20,)),
        ],
        compiler_params=pltpu.CompilerParams(
            collective_id=0, has_side_effects=True, vmem_limit_bytes=40 * 1024 * 1024
        ),
        cost_estimate=pl.CostEstimate(flops=3221225472, bytes_accessed=4 << 20, transcendentals=0),
    )(*arrays)
    return out.reshape(64, 32, CP)


def solution(mesh):
    return jax.shard_map(
        on_device,
        mesh=mesh,
        in_specs=(P(None, ("row", "col"), None), P("row", "col", None), P(), P()),
        out_specs=P("row", "col", None),
        check_vma=False,
    )
```

```python
import jax
import jax.numpy as jnp
from jax import lax
from jax.experimental import pallas as pl
from jax.experimental.pallas import tpu as pltpu
from jax.sharding import PartitionSpec as P

C, CP, S = 32, 128, 512
MESH = pl.DeviceIdType.MESH
PARTS = {"l": ((0, 3), (3, 5)), "r": ((0, 3), (3, 5))}
AROUND = {"l": (1,), "r": (1,)}
NT = (((1,), (1,)), ((), ()))


def ranged(start, size):
    return pl.ds(pl.multiple_of(start, size), size)


def swap_halves(block):
    count = block.shape[0] // 64
    return jnp.concatenate([block[64 * (k ^ 1):64 * (k ^ 1) + 64] for k in range(count)], axis=0)


def product(a, b):
    return lax.dot_general(a, b, NT, preferred_element_type=jnp.float32)


def kernel(lt_hbm, rt_hbm, w_hbm, bias_hbm, out_ref,
           lg, rp, rall, lt_v, rt_v, w_v, bias_v, wp, wide, pb, wb, acc,
           local_sems, ls, lr, rs, rr, ss, sr):
    row, col = lax.axis_index("row"), lax.axis_index("col")
    x, yl = row // 2, row % 2
    yh, z, c = col // 8, (col // 2) % 4, col % 2

    def dev(dx=0, dyl=0, dyh=0, dz=0, dc=0):
        xx, zz = (x + dx + 4) % 4, (z + dz + 4) % 4
        yyl = 1 - yl if dyl else yl
        yyh = 1 - yh if dyh else yh
        cc = 1 - c if dc else c
        return (xx * 2 + yyl, (yyh * 4 + zz) * 2 + cc)

    def slot(kind, p=0, d=0, part=None):
        size = 128 if kind == "l" else 512
        index = dev(dyh=p, dz=d)[1] if kind == "l" else dev(dyl=p, dx=d)[0]
        buffer = lg if kind == "l" else rp
        if part is None:
            return buffer.at[ranged(index * size, size), :]
        first, count = PARTS[kind][part]
        step = size // 8
        return buffer.at[pl.ds(pl.multiple_of(index * size + first * step, step), count * step), :]

    load_l = pltpu.make_async_copy(lt_hbm, lt_v, local_sems.at[0])
    load_r = pltpu.make_async_copy(rt_hbm, rt_v, local_sems.at[1])
    load_w = pltpu.make_async_copy(w_hbm, w_v, local_sems.at[2])
    load_b = pltpu.make_async_copy(bias_hbm, bias_v, local_sems.at[3])
    for load in (load_l, load_r, load_w, load_b):
        load.start()

    barrier = pltpu.get_barrier_semaphore()
    peers = [dev(dx=1), dev(dx=-1), dev(dx=2), dev(dyl=1), dev(dyh=1),
             dev(dz=1), dev(dz=-1), dev(dz=2), dev(dc=1)]
    for peer in peers:
        pl.semaphore_signal(barrier, inc=1, device_id=peer, device_id_type=MESH)

    def interleave(a, b):
        low = lax.broadcasted_iota(jnp.int32, a.shape, 1) < 64
        return jnp.where(low, a, pltpu.roll(b, 64, 1)), jnp.where(low, pltpu.roll(a, 64, 1), b)

    load_l.wait()
    own_l = ranged(col * 128, 128)
    for t in range(2):
        even, odd = interleave(lt_v[:, t * 256:t * 256 + 128], lt_v[:, t * 256 + 128:t * 256 + 256])
        lg[own_l, t * 128:t * 128 + 128] = even
        lg[own_l, 256 + t * 128:256 + t * 128 + 128] = odd
    lane_f = lax.broadcasted_iota(jnp.int32, (32, 128), 1)

    def prepare_right():
        load_r.wait()
        wide[:, 0:64] = rt_v[...].astype(jnp.float32)
        for e in range(16):
            lo = wide[pl.ds(e, 32, stride=32), :]
            hi = wide[pl.ds(e + 16, 32, stride=32), :]
            both = jnp.where(lane_f < 64, lo, pltpu.roll(hi, 64, 1))
            rp[ranged(row * 512 + e * 32, 32), :] = both.astype(jnp.bfloat16)

    def prepare_weight():
        load_w.wait()
        load_b.wait()
        wide[...] = w_v[...].astype(jnp.float32)
        for e in range(32):
            wp[pl.ds(e * 32, 32), :] = wide[pl.ds(e, 32, stride=32), :].astype(jnp.bfloat16)
        zero = jnp.zeros((32, 128), jnp.bfloat16)
        for side in range(2):
            for e in range(16):
                for h in range(2):
                    source = (e + 16 * (h ^ side)) * 32
                    block = wp[source:source + 32, :]
                    for i2 in range(2):
                        r = side * 2048 + e * 128 + h * 64 + i2 * 32
                        wb[r:r + 32, i2 * 128:i2 * 128 + 128] = block
                        wb[r:r + 32, (1 - i2) * 128:(1 - i2) * 128 + 128] = zero

    def mover(send, recv):
        started = []

        def move(ref, to):
            k = len(started)
            copy = pltpu.make_async_remote_copy(
                src_ref=ref, dst_ref=ref, send_sem=send.at[k], recv_sem=recv.at[k],
                device_id=to, device_id_type=MESH)
            copy.start()
            started.append(copy)
            return copy
        return move, started

    lmove, lsent = mover(ls, lr)
    rmove, rsent = mover(rs, rr)
    smove, ssent = mover(ss, sr)
    move = {"l": lmove, "r": rmove}
    to = {"l": {"up": dev(dz=1), "down": dev(dz=-1), "far": dev(dz=2), "pair": dev(dyh=1)},
          "r": {"up": dev(dx=1), "down": dev(dx=-1), "far": dev(dx=2), "pair": dev(dyl=1)}}
    sib = dev(dc=1)
    parts = {kind: range(len(PARTS[kind])) for kind in PARTS}
    most = range(max(len(parts["l"]), len(parts["r"])))
    ways = ("far", "up", "down")
    came = {"up": -1, "down": 1, "far": 2}
    g = {}
    sibs = {}

    def share(p, d, k=None):
        sibs[p, d, k] = smove(slot("l", p, d, k), sib)

    def send_pair(kind, k):
        g[kind, "pair", k] = move[kind](slot(kind, 0, 0, k), to[kind]["pair"])

    def send_own(kind, way, k=None):
        key = (kind, way, 0) if k is None else (kind, way, 0, k)
        g[key] = move[kind](slot(kind, 0, 0, k), to[kind][way])

    def send_on(kind, k):
        g[kind, "pair", k].wait_recv()
        for way in ways:
            if way != "far" or k not in AROUND[kind]:
                g[kind, way, 1, k] = move[kind](slot(kind, 1, 0, k), to[kind][way])

    def send_around(kind, k):
        g[kind, "far", 0, k].wait_recv()
        g[kind, "far", 1, k] = move[kind](slot(kind, 0, 2, k), to[kind]["pair"])

    prepare_right()
    pl.semaphore_wait(barrier, len(peers))
    for kind in ("l", "r"):
        for k in parts[kind]:
            send_pair(kind, k)
    for kind in ("l", "r"):
        for k in sorted(parts[kind], key=lambda k: k not in AROUND[kind]):
            send_own(kind, "far", k)
    for way in ("up", "down"):
        send_own("l", way)
        send_own("r", way)
    share(0, 0)
    prepare_weight()

    def unpack(m):
        parity = yl if m == 0 else 1 - yl
        for t in range(2):
            a = rp[ranged((4 * t + parity) * 512, 512), :]
            b = rp[ranged((4 * t + 2 + parity) * 512, 512), :]
            low, high = interleave(a, b)
            rall[0:512, m * 256 + t * 128:m * 256 + t * 128 + 128] = low
            rall[512:1024, m * 256 + t * 128:m * 256 + t * 128 + 128] = high

    lanes = [ranged(yl * 256, 256), ranged((1 - yl) * 256, 256)]
    lowlane = lax.broadcasted_iota(jnp.int32, (512, 256), 1) % 128 < 64

    def mix(o_lo, o_hi, rows):
        o_lo, o_hi = o_lo.astype(jnp.bfloat16), o_hi.astype(jnp.bfloat16)
        for side, mixed in enumerate((jnp.where(lowlane, o_lo, o_hi), jnp.where(lowlane, o_hi, o_lo))):
            for e in range(16):
                for t, r in enumerate(rows):
                    pb[side, r:r + 32, e * 128:e * 128 + 128] = mixed[e * 32:e * 32 + 32, t * 128:t * 128 + 128]

    def project(first, blocks):
        count = 32 * len(blocks)
        for side in range(2):
            res = jnp.dot(pb[side, first:first + count, :], wb[side * 2048:side * 2048 + 2048, :],
                          preferred_element_type=jnp.float32)
            for t, b in enumerate(blocks):
                for i2 in range(2):
                    out_ref[ranged(b * 128 + (2 * side + i2) * 32, 32), :] = (
                        res[t * 32:t * 32 + 32, i2 * 128:i2 * 128 + 128] * (1.0 / S) + bias_v[...])

    for k in most:
        for kind in ("l", "r"):
            if k in parts[kind]:
                send_on(kind, k)
    for kind in ("l", "r"):
        for k in AROUND[kind]:
            send_around(kind, k)
    share(1, 0)
    for way in ways:
        for kind in ("l", "r"):
            if way == "far":
                for k in parts[kind]:
                    if k not in AROUND[kind]:
                        g[kind, way, 0, k].wait_recv()
            else:
                g[kind, way, 0].wait_recv()
            if kind == "l":
                share(0, came[way])
    for d in (0, 2, -1, 1):
        sibs[0, d, None].wait_recv()
    unpack(0)
    for t in range(4):
        block = lg[ranged(yh * 1024 + t * 256, 256), lanes[0]]
        acc[2 * t] = product(rall[0:512, 0:256], block)
        acc[2 * t + 1] = product(rall[512:1024, 0:256], swap_halves(block))

    def pass_on(k):
        for way in ways:
            g["l", way, 1, k].wait_recv()
            share(1, came[way], k)

    def finish(t):
        block = lg[ranged(yh * 1024 + t * 256, 256), lanes[1]]
        mix(acc[2 * t] + product(rall[0:512, 256:512], block),
            acc[2 * t + 1] + product(rall[512:1024, 256:512], swap_halves(block)),
            (t * 64, t * 64 + 32))

    for k in parts["l"]:
        pass_on(k)
    for k in parts["r"]:
        for way in ways:
            g["r", way, 1, k].wait_recv()
    unpack(1)
    for t in range(0):
        finish(t)
    for t in range(0, 4):
        finish(t)
    project(0, [yh * 8 + t for t in range(8)])

    other = (1 - yh) * 8
    for who in range(2):
        core = c if who == 0 else 1 - c
        if who == 1:
            sibs[1, 0, None].wait_recv()
            for k in parts["l"]:
                for d in (2, -1, 1):
                    sibs[1, d, k].wait_recv()
        for t in range(2):
            block = jnp.concatenate(
                [jnp.concatenate([lg[ranged((other + (2 * t + u) * 2 + core) * 128, 128), lanes[m]] for m in range(2)], axis=1)
                 for u in range(2)], axis=0)
            r = 256 + who * 128 + t * 64
            mix(product(rall[0:512, :], block), product(rall[512:1024, :], swap_halves(block)), (r, r + 32))
        project(256 + who * 128, [other + t * 2 + core for t in range(4)])
    for copy in lsent + rsent + ssent:
        copy.wait_send()


def on_device(left_act, right_act, proj_weight, proj_bias):
    lt = jnp.transpose(left_act, (1, 2, 0)).reshape(128, S)
    rt = jnp.transpose(right_act, (1, 2, 0)).reshape(1024, 64)
    bias = proj_bias.reshape(1, CP)
    hbm, vmem = pl.BlockSpec(memory_space=pltpu.HBM), pl.BlockSpec(memory_space=pltpu.VMEM)
    dma = pltpu.SemaphoreType.DMA
    arrays = [pltpu.with_memory_space_constraint(a, pltpu.HBM) for a in (lt, rt, proj_weight, bias)]
    out = pl.pallas_call(
        kernel,
        out_shape=jax.ShapeDtypeStruct((2048, CP), jnp.float32),
        in_specs=[hbm, hbm, hbm, hbm],
        out_specs=vmem,
        scratch_shapes=[
            pltpu.VMEM((2048, S), jnp.bfloat16),
            pltpu.VMEM((4096, 128), jnp.bfloat16),
            pltpu.VMEM((1024, S), jnp.bfloat16),
            pltpu.VMEM((128, S), jnp.bfloat16),
            pltpu.VMEM((1024, 64), jnp.bfloat16),
            pltpu.VMEM((1024, 128), jnp.bfloat16),
            pltpu.VMEM((1, 128), jnp.float32),
            pltpu.VMEM((1024, 128), jnp.bfloat16),
            pltpu.VMEM((1024, 128), jnp.float32),
            pltpu.VMEM((2, 512, 2048), jnp.bfloat16),
            pltpu.VMEM((4096, 256), jnp.bfloat16),
            pltpu.VMEM((8, 512, 256), jnp.float32),
            dma((4,)), dma((20,)), dma((20,)), dma((20,)), dma((20,)), dma((20,)), dma((20,)),
        ],
        compiler_params=pltpu.CompilerParams(
            collective_id=0, has_side_effects=True, vmem_limit_bytes=40 * 1024 * 1024
        ),
        cost_estimate=pl.CostEstimate(flops=3221225472, bytes_accessed=4 << 20, transcendentals=0),
    )(*arrays)
    return out.reshape(64, 32, CP)


def solution(mesh):
    return jax.shard_map(
        on_device,
        mesh=mesh,
        in_specs=(P(None, ("row", "col"), None), P("row", "col", None), P(), P()),
        out_specs=P("row", "col", None),
        check_vma=False,
    )
```

```python
import jax
import jax.numpy as jnp
from jax import lax
from jax.experimental import pallas as pl
from jax.experimental.pallas import tpu as pltpu
from jax.sharding import PartitionSpec as P

C, CP, S = 32, 128, 512
MESH = pl.DeviceIdType.MESH
PARTS = {"l": ((0, 3), (3, 5)), "r": ((0, 3), (3, 5))}
AROUND = {"l": (1,), "r": (1,)}
NT = (((1,), (1,)), ((), ()))


def ranged(start, size):
    return pl.ds(pl.multiple_of(start, size), size)


def swap_halves(block):
    count = block.shape[0] // 64
    return jnp.concatenate([block[64 * (k ^ 1):64 * (k ^ 1) + 64] for k in range(count)], axis=0)


def product(a, b):
    return lax.dot_general(a, b, NT, preferred_element_type=jnp.float32)


def kernel(lt_hbm, rt_hbm, w_hbm, bias_hbm, out_ref,
           lg, rp, rall, lt_v, rt_v, w_v, bias_v, wp, wide, pb, wb, acc,
           local_sems, ls, lr, rs, rr, ss, sr):
    row, col = lax.axis_index("row"), lax.axis_index("col")
    x, yl = row // 2, row % 2
    yh, z, c = col // 8, (col // 2) % 4, col % 2

    def dev(dx=0, dyl=0, dyh=0, dz=0, dc=0):
        xx, zz = (x + dx + 4) % 4, (z + dz + 4) % 4
        yyl = 1 - yl if dyl else yl
        yyh = 1 - yh if dyh else yh
        cc = 1 - c if dc else c
        return (xx * 2 + yyl, (yyh * 4 + zz) * 2 + cc)

    def slot(kind, p=0, d=0, part=None):
        size = 128 if kind == "l" else 512
        index = dev(dyh=p, dz=d)[1] if kind == "l" else dev(dyl=p, dx=d)[0]
        buffer = lg if kind == "l" else rp
        if part is None:
            return buffer.at[ranged(index * size, size), :]
        first, count = PARTS[kind][part]
        step = size // 8
        return buffer.at[pl.ds(pl.multiple_of(index * size + first * step, step), count * step), :]

    load_l = pltpu.make_async_copy(lt_hbm, lt_v, local_sems.at[0])
    load_r = pltpu.make_async_copy(rt_hbm, rt_v, local_sems.at[1])
    load_w = pltpu.make_async_copy(w_hbm, w_v, local_sems.at[2])
    load_b = pltpu.make_async_copy(bias_hbm, bias_v, local_sems.at[3])
    for load in (load_l, load_r, load_w, load_b):
        load.start()

    barrier = pltpu.get_barrier_semaphore()
    peers = [dev(dx=1), dev(dx=-1), dev(dx=2), dev(dyl=1), dev(dyh=1),
             dev(dz=1), dev(dz=-1), dev(dz=2), dev(dc=1)]
    for peer in peers:
        pl.semaphore_signal(barrier, inc=1, device_id=peer, device_id_type=MESH)

    def interleave(a, b):
        low = lax.broadcasted_iota(jnp.int32, a.shape, 1) < 64
        return jnp.where(low, a, pltpu.roll(b, 64, 1)), jnp.where(low, pltpu.roll(a, 64, 1), b)

    load_l.wait()
    own_l = ranged(col * 128, 128)
    for t in range(2):
        even, odd = interleave(lt_v[:, t * 256:t * 256 + 128], lt_v[:, t * 256 + 128:t * 256 + 256])
        lg[own_l, t * 128:t * 128 + 128] = even
        lg[own_l, 256 + t * 128:256 + t * 128 + 128] = odd
    lane_f = lax.broadcasted_iota(jnp.int32, (32, 128), 1)

    def prepare_right():
        load_r.wait()
        wide[:, 0:64] = rt_v[...].astype(jnp.float32)
        for e in range(16):
            lo = wide[pl.ds(e, 32, stride=32), :]
            hi = wide[pl.ds(e + 16, 32, stride=32), :]
            both = jnp.where(lane_f < 64, lo, pltpu.roll(hi, 64, 1))
            rp[ranged(row * 512 + e * 32, 32), :] = both.astype(jnp.bfloat16)

    def prepare_weight():
        load_w.wait()
        load_b.wait()
        wide[...] = w_v[...].astype(jnp.float32)
        for e in range(32):
            wp[pl.ds(e * 32, 32), :] = wide[pl.ds(e, 32, stride=32), :].astype(jnp.bfloat16)
        zero = jnp.zeros((32, 128), jnp.bfloat16)
        for side in range(2):
            for e in range(16):
                for h in range(2):
                    source = (e + 16 * (h ^ side)) * 32
                    block = wp[source:source + 32, :]
                    for i2 in range(2):
                        r = side * 2048 + e * 128 + h * 64 + i2 * 32
                        wb[r:r + 32, i2 * 128:i2 * 128 + 128] = block
                        wb[r:r + 32, (1 - i2) * 128:(1 - i2) * 128 + 128] = zero

    def mover(send, recv):
        started = []

        def move(ref, to):
            k = len(started)
            copy = pltpu.make_async_remote_copy(
                src_ref=ref, dst_ref=ref, send_sem=send.at[k], recv_sem=recv.at[k],
                device_id=to, device_id_type=MESH)
            copy.start()
            started.append(copy)
            return copy
        return move, started

    lmove, lsent = mover(ls, lr)
    rmove, rsent = mover(rs, rr)
    smove, ssent = mover(ss, sr)
    move = {"l": lmove, "r": rmove}
    to = {"l": {"up": dev(dz=1), "down": dev(dz=-1), "far": dev(dz=2), "pair": dev(dyh=1)},
          "r": {"up": dev(dx=1), "down": dev(dx=-1), "far": dev(dx=2), "pair": dev(dyl=1)}}
    sib = dev(dc=1)
    parts = {kind: range(len(PARTS[kind])) for kind in PARTS}
    most = range(max(len(parts["l"]), len(parts["r"])))
    ways = ("far", "up", "down")
    came = {"up": -1, "down": 1, "far": 2}
    g = {}
    sibs = {}

    def share(p, d, k=None):
        sibs[p, d, k] = smove(slot("l", p, d, k), sib)

    def send_pair(kind, k):
        g[kind, "pair", k] = move[kind](slot(kind, 0, 0, k), to[kind]["pair"])

    def send_own(kind, way, k=None):
        key = (kind, way, 0) if k is None else (kind, way, 0, k)
        g[key] = move[kind](slot(kind, 0, 0, k), to[kind][way])

    def send_on(kind, k):
        g[kind, "pair", k].wait_recv()
        for way in ways:
            if way != "far" or k not in AROUND[kind]:
                g[kind, way, 1, k] = move[kind](slot(kind, 1, 0, k), to[kind][way])

    def send_around(kind, k):
        g[kind, "far", 0, k].wait_recv()
        g[kind, "far", 1, k] = move[kind](slot(kind, 0, 2, k), to[kind]["pair"])

    prepare_right()
    pl.semaphore_wait(barrier, len(peers))
    for kind in ("l", "r"):
        for k in parts[kind]:
            send_pair(kind, k)
    for kind in ("l", "r"):
        for k in sorted(parts[kind], key=lambda k: k not in AROUND[kind]):
            send_own(kind, "far", k)
    for way in ("up", "down"):
        send_own("l", way)
        send_own("r", way)
    share(0, 0)
    prepare_weight()

    def unpack(m):
        parity = yl if m == 0 else 1 - yl
        for t in range(2):
            a = rp[ranged((4 * t + parity) * 512, 512), :]
            b = rp[ranged((4 * t + 2 + parity) * 512, 512), :]
            low, high = interleave(a, b)
            rall[0:512, m * 256 + t * 128:m * 256 + t * 128 + 128] = low
            rall[512:1024, m * 256 + t * 128:m * 256 + t * 128 + 128] = high

    lanes = [ranged(yl * 256, 256), ranged((1 - yl) * 256, 256)]
    lowlane = lax.broadcasted_iota(jnp.int32, (512, 256), 1) % 128 < 64

    def mix(o_lo, o_hi, rows):
        o_lo, o_hi = o_lo.astype(jnp.bfloat16), o_hi.astype(jnp.bfloat16)
        for side, mixed in enumerate((jnp.where(lowlane, o_lo, o_hi), jnp.where(lowlane, o_hi, o_lo))):
            for e in range(16):
                for t, r in enumerate(rows):
                    pb[side, r:r + 32, e * 128:e * 128 + 128] = mixed[e * 32:e * 32 + 32, t * 128:t * 128 + 128]

    def project(first, blocks):
        count = 32 * len(blocks)
        for side in range(2):
            res = jnp.dot(pb[side, first:first + count, :], wb[side * 2048:side * 2048 + 2048, :],
                          preferred_element_type=jnp.float32)
            for t, b in enumerate(blocks):
                for i2 in range(2):
                    out_ref[ranged(b * 128 + (2 * side + i2) * 32, 32), :] = (
                        res[t * 32:t * 32 + 32, i2 * 128:i2 * 128 + 128] * (1.0 / S) + bias_v[...])

    for k in most:
        for kind in ("l", "r"):
            if k in parts[kind]:
                send_on(kind, k)
    for kind in ("l", "r"):
        for k in AROUND[kind]:
            send_around(kind, k)
    share(1, 0)
    for way in ways:
        for kind in ("l", "r"):
            if way == "far":
                for k in parts[kind]:
                    if k not in AROUND[kind]:
                        g[kind, way, 0, k].wait_recv()
            else:
                g[kind, way, 0].wait_recv()
            if kind == "l":
                share(0, came[way])
    for d in (0, 2, -1, 1):
        sibs[0, d, None].wait_recv()
    unpack(0)
    for t in range(4):
        block = lg[ranged(yh * 1024 + t * 256, 256), lanes[0]]
        acc[2 * t] = product(rall[0:512, 0:256], block)
        acc[2 * t + 1] = product(rall[512:1024, 0:256], swap_halves(block))

    def pass_on(way, k):
        g["l", way, 1, k].wait_recv()
        share(1, came[way], k)

    def finish(t):
        block = lg[ranged(yh * 1024 + t * 256, 256), lanes[1]]
        mix(acc[2 * t] + product(rall[0:512, 256:512], block),
            acc[2 * t + 1] + product(rall[512:1024, 256:512], swap_halves(block)),
            (t * 64, t * 64 + 32))

    for way, k in (("far", 0), ("far", 1), ("up", 0), ("down", 0), ("up", 1), ("down", 1)):
        pass_on(way, k)
    for k in parts["r"]:
        for way in ways:
            g["r", way, 1, k].wait_recv()
    unpack(1)
    for t in range(0):
        finish(t)
    for t in range(0, 4):
        finish(t)
    project(0, [yh * 8 + t for t in range(8)])

    other = (1 - yh) * 8
    for who in range(2):
        core = c if who == 0 else 1 - c
        if who == 1:
            sibs[1, 0, None].wait_recv()
            for k in parts["l"]:
                for d in (2, -1, 1):
                    sibs[1, d, k].wait_recv()
        for t in range(2):
            block = jnp.concatenate(
                [jnp.concatenate([lg[ranged((other + (2 * t + u) * 2 + core) * 128, 128), lanes[m]] for m in range(2)], axis=1)
                 for u in range(2)], axis=0)
            r = 256 + who * 128 + t * 64
            mix(product(rall[0:512, :], block), product(rall[512:1024, :], swap_halves(block)), (r, r + 32))
        project(256 + who * 128, [other + t * 2 + core for t in range(4)])
    for copy in lsent + rsent + ssent:
        copy.wait_send()


def on_device(left_act, right_act, proj_weight, proj_bias):
    lt = jnp.transpose(left_act, (1, 2, 0)).reshape(128, S)
    rt = jnp.transpose(right_act, (1, 2, 0)).reshape(1024, 64)
    bias = proj_bias.reshape(1, CP)
    hbm, vmem = pl.BlockSpec(memory_space=pltpu.HBM), pl.BlockSpec(memory_space=pltpu.VMEM)
    dma = pltpu.SemaphoreType.DMA
    arrays = [pltpu.with_memory_space_constraint(a, pltpu.HBM) for a in (lt, rt, proj_weight, bias)]
    out = pl.pallas_call(
        kernel,
        out_shape=jax.ShapeDtypeStruct((2048, CP), jnp.float32),
        in_specs=[hbm, hbm, hbm, hbm],
        out_specs=vmem,
        scratch_shapes=[
            pltpu.VMEM((2048, S), jnp.bfloat16),
            pltpu.VMEM((4096, 128), jnp.bfloat16),
            pltpu.VMEM((1024, S), jnp.bfloat16),
            pltpu.VMEM((128, S), jnp.bfloat16),
            pltpu.VMEM((1024, 64), jnp.bfloat16),
            pltpu.VMEM((1024, 128), jnp.bfloat16),
            pltpu.VMEM((1, 128), jnp.float32),
            pltpu.VMEM((1024, 128), jnp.bfloat16),
            pltpu.VMEM((1024, 128), jnp.float32),
            pltpu.VMEM((2, 512, 2048), jnp.bfloat16),
            pltpu.VMEM((4096, 256), jnp.bfloat16),
            pltpu.VMEM((8, 512, 256), jnp.float32),
            dma((4,)), dma((20,)), dma((20,)), dma((20,)), dma((20,)), dma((20,)), dma((20,)),
        ],
        compiler_params=pltpu.CompilerParams(
            collective_id=0, has_side_effects=True, vmem_limit_bytes=40 * 1024 * 1024
        ),
        cost_estimate=pl.CostEstimate(flops=3221225472, bytes_accessed=4 << 20, transcendentals=0),
    )(*arrays)
    return out.reshape(64, 32, CP)


def solution(mesh):
    return jax.shard_map(
        on_device,
        mesh=mesh,
        in_specs=(P(None, ("row", "col"), None), P("row", "col", None), P(), P()),
        out_specs=P("row", "col", None),
        check_vma=False,
    )
```

```python
import jax
import jax.numpy as jnp
from jax import lax
from jax.experimental import pallas as pl
from jax.experimental.pallas import tpu as pltpu
from jax.sharding import PartitionSpec as P

C, CP, S = 32, 128, 512
MESH = pl.DeviceIdType.MESH
PARTS = {"l": ((0, 3), (3, 5)), "r": ((0, 3), (3, 5))}
AROUND = {"l": (1,), "r": (1,)}
NT = (((1,), (1,)), ((), ()))


def ranged(start, size):
    return pl.ds(pl.multiple_of(start, size), size)


def swap_halves(block):
    count = block.shape[0] // 64
    return jnp.concatenate([block[64 * (k ^ 1):64 * (k ^ 1) + 64] for k in range(count)], axis=0)


def product(a, b):
    return lax.dot_general(a, b, NT, preferred_element_type=jnp.float32)


def kernel(lt_hbm, rt_hbm, w_hbm, bias_hbm, out_ref,
           lg, rp, rall, lt_v, rt_v, w_v, bias_v, wp, wide, pb, wb, acc,
           local_sems, ls, lr, rs, rr, ss, sr):
    row, col = lax.axis_index("row"), lax.axis_index("col")
    x, yl = row // 2, row % 2
    yh, z, c = col // 8, (col // 2) % 4, col % 2

    def dev(dx=0, dyl=0, dyh=0, dz=0, dc=0):
        xx, zz = (x + dx + 4) % 4, (z + dz + 4) % 4
        yyl = 1 - yl if dyl else yl
        yyh = 1 - yh if dyh else yh
        cc = 1 - c if dc else c
        return (xx * 2 + yyl, (yyh * 4 + zz) * 2 + cc)

    def slot(kind, p=0, d=0, part=None):
        size = 128 if kind == "l" else 512
        index = dev(dyh=p, dz=d)[1] if kind == "l" else dev(dyl=p, dx=d)[0]
        buffer = lg if kind == "l" else rp
        if part is None:
            return buffer.at[ranged(index * size, size), :]
        first, count = PARTS[kind][part]
        step = size // 8
        return buffer.at[pl.ds(pl.multiple_of(index * size + first * step, step), count * step), :]

    load_l = pltpu.make_async_copy(lt_hbm, lt_v, local_sems.at[0])
    load_r = pltpu.make_async_copy(rt_hbm, rt_v, local_sems.at[1])
    load_w = pltpu.make_async_copy(w_hbm, w_v, local_sems.at[2])
    load_b = pltpu.make_async_copy(bias_hbm, bias_v, local_sems.at[3])
    for load in (load_l, load_r, load_w, load_b):
        load.start()

    barrier = pltpu.get_barrier_semaphore()
    peers = [dev(dx=1), dev(dx=-1), dev(dx=2), dev(dyl=1), dev(dyh=1),
             dev(dz=1), dev(dz=-1), dev(dz=2), dev(dc=1)]
    for peer in peers:
        pl.semaphore_signal(barrier, inc=1, device_id=peer, device_id_type=MESH)

    def interleave(a, b):
        low = lax.broadcasted_iota(jnp.int32, a.shape, 1) < 64
        return jnp.where(low, a, pltpu.roll(b, 64, 1)), jnp.where(low, pltpu.roll(a, 64, 1), b)

    load_l.wait()
    own_l = ranged(col * 128, 128)
    for t in range(2):
        even, odd = interleave(lt_v[:, t * 256:t * 256 + 128], lt_v[:, t * 256 + 128:t * 256 + 256])
        lg[own_l, t * 128:t * 128 + 128] = even
        lg[own_l, 256 + t * 128:256 + t * 128 + 128] = odd
    lane_f = lax.broadcasted_iota(jnp.int32, (32, 128), 1)

    def prepare_right():
        load_r.wait()
        wide[:, 0:64] = rt_v[...].astype(jnp.float32)
        for e in range(16):
            lo = wide[pl.ds(e, 32, stride=32), :]
            hi = wide[pl.ds(e + 16, 32, stride=32), :]
            both = jnp.where(lane_f < 64, lo, pltpu.roll(hi, 64, 1))
            rp[ranged(row * 512 + e * 32, 32), :] = both.astype(jnp.bfloat16)

    def prepare_weight():
        load_w.wait()
        load_b.wait()
        wide[...] = w_v[...].astype(jnp.float32)
        for e in range(32):
            wp[pl.ds(e * 32, 32), :] = wide[pl.ds(e, 32, stride=32), :].astype(jnp.bfloat16)
        zero = jnp.zeros((32, 128), jnp.bfloat16)
        for side in range(2):
            for e in range(16):
                for h in range(2):
                    source = (e + 16 * (h ^ side)) * 32
                    block = wp[source:source + 32, :]
                    for i2 in range(2):
                        r = side * 2048 + e * 128 + h * 64 + i2 * 32
                        wb[r:r + 32, i2 * 128:i2 * 128 + 128] = block
                        wb[r:r + 32, (1 - i2) * 128:(1 - i2) * 128 + 128] = zero

    def mover(send, recv):
        started = []

        def move(ref, to):
            k = len(started)
            copy = pltpu.make_async_remote_copy(
                src_ref=ref, dst_ref=ref, send_sem=send.at[k], recv_sem=recv.at[k],
                device_id=to, device_id_type=MESH)
            copy.start()
            started.append(copy)
            return copy
        return move, started

    lmove, lsent = mover(ls, lr)
    rmove, rsent = mover(rs, rr)
    smove, ssent = mover(ss, sr)
    move = {"l": lmove, "r": rmove}
    to = {"l": {"up": dev(dz=1), "down": dev(dz=-1), "far": dev(dz=2), "pair": dev(dyh=1)},
          "r": {"up": dev(dx=1), "down": dev(dx=-1), "far": dev(dx=2), "pair": dev(dyl=1)}}
    sib = dev(dc=1)
    parts = {kind: range(len(PARTS[kind])) for kind in PARTS}
    most = range(max(len(parts["l"]), len(parts["r"])))
    ways = ("far", "up", "down")
    came = {"up": -1, "down": 1, "far": 2}
    g = {}
    sibs = {}

    def share(p, d, k=None):
        sibs[p, d, k] = smove(slot("l", p, d, k), sib)

    def send_pair(kind, k):
        g[kind, "pair", k] = move[kind](slot(kind, 0, 0, k), to[kind]["pair"])

    def send_own(kind, way, k=None):
        key = (kind, way, 0) if k is None else (kind, way, 0, k)
        g[key] = move[kind](slot(kind, 0, 0, k), to[kind][way])

    def send_on(kind, k):
        g[kind, "pair", k].wait_recv()
        for way in ways:
            if way != "far" or k not in AROUND[kind]:
                g[kind, way, 1, k] = move[kind](slot(kind, 1, 0, k), to[kind][way])

    def send_around(kind, k):
        g[kind, "far", 0, k].wait_recv()
        g[kind, "far", 1, k] = move[kind](slot(kind, 0, 2, k), to[kind]["pair"])

    prepare_right()
    pl.semaphore_wait(barrier, len(peers))
    for kind in ("l", "r"):
        for k in parts[kind]:
            send_pair(kind, k)
    for kind in ("l", "r"):
        for k in sorted(parts[kind], key=lambda k: k not in AROUND[kind]):
            send_own(kind, "far", k)
    for way in ("up", "down"):
        send_own("l", way)
        send_own("r", way)
    share(0, 0)
    prepare_weight()

    def unpack(m):
        parity = yl if m == 0 else 1 - yl
        for t in range(2):
            a = rp[ranged((4 * t + parity) * 512, 512), :]
            b = rp[ranged((4 * t + 2 + parity) * 512, 512), :]
            low, high = interleave(a, b)
            rall[0:512, m * 256 + t * 128:m * 256 + t * 128 + 128] = low
            rall[512:1024, m * 256 + t * 128:m * 256 + t * 128 + 128] = high

    lanes = [ranged(yl * 256, 256), ranged((1 - yl) * 256, 256)]
    lowlane = lax.broadcasted_iota(jnp.int32, (512, 256), 1) % 128 < 64

    def mix(o_lo, o_hi, rows):
        o_lo, o_hi = o_lo.astype(jnp.bfloat16), o_hi.astype(jnp.bfloat16)
        for side, mixed in enumerate((jnp.where(lowlane, o_lo, o_hi), jnp.where(lowlane, o_hi, o_lo))):
            for e in range(16):
                for t, r in enumerate(rows):
                    pb[side, r:r + 32, e * 128:e * 128 + 128] = mixed[e * 32:e * 32 + 32, t * 128:t * 128 + 128]

    def project(first, blocks):
        count = 32 * len(blocks)
        for side in range(2):
            res = jnp.dot(pb[side, first:first + count, :], wb[side * 2048:side * 2048 + 2048, :],
                          preferred_element_type=jnp.float32)
            for t, b in enumerate(blocks):
                for i2 in range(2):
                    out_ref[ranged(b * 128 + (2 * side + i2) * 32, 32), :] = (
                        res[t * 32:t * 32 + 32, i2 * 128:i2 * 128 + 128] * (1.0 / S) + bias_v[...])

    for k in most:
        for kind in ("l", "r"):
            if k in parts[kind]:
                send_on(kind, k)
    for kind in ("l", "r"):
        for k in AROUND[kind]:
            send_around(kind, k)
    share(1, 0)
    for way in ways:
        for kind in ("l", "r"):
            if way == "far":
                for k in parts[kind]:
                    if k not in AROUND[kind]:
                        g[kind, way, 0, k].wait_recv()
            else:
                g[kind, way, 0].wait_recv()
            if kind == "l":
                share(0, came[way])
    for d in (0, 2, -1, 1):
        sibs[0, d, None].wait_recv()
    unpack(0)
    for t in range(4):
        block = lg[ranged(yh * 1024 + t * 256, 256), lanes[0]]
        acc[2 * t] = product(rall[0:512, 0:256], block)
        acc[2 * t + 1] = product(rall[512:1024, 0:256], swap_halves(block))

    def pass_on(k):
        for way in ways:
            g["l", way, 1, k].wait_recv()
            share(1, came[way], k)

    def finish(t):
        block = lg[ranged(yh * 1024 + t * 256, 256), lanes[1]]
        mix(acc[2 * t] + product(rall[0:512, 256:512], block),
            acc[2 * t + 1] + product(rall[512:1024, 256:512], swap_halves(block)),
            (t * 64, t * 64 + 32))

    early = [g[key] for key in g if key[1] == "pair" or key[2] == 0] + [sibs[key] for key in sibs if key[0] == 0]
    left = {id(copy) for copy in early}
    for copy in early:
        copy.wait_send()
    for k in parts["l"]:
        pass_on(k)
    for k in parts["r"]:
        for way in ways:
            g["r", way, 1, k].wait_recv()
    unpack(1)
    for t in range(0):
        finish(t)
    for t in range(0, 4):
        finish(t)
    project(0, [yh * 8 + t for t in range(8)])

    other = (1 - yh) * 8
    for who in range(2):
        core = c if who == 0 else 1 - c
        if who == 1:
            sibs[1, 0, None].wait_recv()
            for k in parts["l"]:
                for d in (2, -1, 1):
                    sibs[1, d, k].wait_recv()
        for t in range(2):
            block = jnp.concatenate(
                [jnp.concatenate([lg[ranged((other + (2 * t + u) * 2 + core) * 128, 128), lanes[m]] for m in range(2)], axis=1)
                 for u in range(2)], axis=0)
            r = 256 + who * 128 + t * 64
            mix(product(rall[0:512, :], block), product(rall[512:1024, :], swap_halves(block)), (r, r + 32))
        project(256 + who * 128, [other + t * 2 + core for t in range(4)])
    for copy in lsent + rsent + ssent:
        if id(copy) not in left:
            copy.wait_send()


def on_device(left_act, right_act, proj_weight, proj_bias):
    lt = jnp.transpose(left_act, (1, 2, 0)).reshape(128, S)
    rt = jnp.transpose(right_act, (1, 2, 0)).reshape(1024, 64)
    bias = proj_bias.reshape(1, CP)
    hbm, vmem = pl.BlockSpec(memory_space=pltpu.HBM), pl.BlockSpec(memory_space=pltpu.VMEM)
    dma = pltpu.SemaphoreType.DMA
    arrays = [pltpu.with_memory_space_constraint(a, pltpu.HBM) for a in (lt, rt, proj_weight, bias)]
    out = pl.pallas_call(
        kernel,
        out_shape=jax.ShapeDtypeStruct((2048, CP), jnp.float32),
        in_specs=[hbm, hbm, hbm, hbm],
        out_specs=vmem,
        scratch_shapes=[
            pltpu.VMEM((2048, S), jnp.bfloat16),
            pltpu.VMEM((4096, 128), jnp.bfloat16),
            pltpu.VMEM((1024, S), jnp.bfloat16),
            pltpu.VMEM((128, S), jnp.bfloat16),
            pltpu.VMEM((1024, 64), jnp.bfloat16),
            pltpu.VMEM((1024, 128), jnp.bfloat16),
            pltpu.VMEM((1, 128), jnp.float32),
            pltpu.VMEM((1024, 128), jnp.bfloat16),
            pltpu.VMEM((1024, 128), jnp.float32),
            pltpu.VMEM((2, 512, 2048), jnp.bfloat16),
            pltpu.VMEM((4096, 256), jnp.bfloat16),
            pltpu.VMEM((8, 512, 256), jnp.float32),
            dma((4,)), dma((20,)), dma((20,)), dma((20,)), dma((20,)), dma((20,)), dma((20,)),
        ],
        compiler_params=pltpu.CompilerParams(
            collective_id=0, has_side_effects=True, vmem_limit_bytes=40 * 1024 * 1024
        ),
        cost_estimate=pl.CostEstimate(flops=3221225472, bytes_accessed=4 << 20, transcendentals=0),
    )(*arrays)
    return out.reshape(64, 32, CP)


def solution(mesh):
    return jax.shard_map(
        on_device,
        mesh=mesh,
        in_specs=(P(None, ("row", "col"), None), P("row", "col", None), P(), P()),
        out_specs=P("row", "col", None),
        check_vma=False,
    )
```
